32 devices in a mesh: pairs: 8 (over z, x), vecs: 4 (over y, core).
Axes of the slice: x: 2, y: 2, z: 4, core: 2. Of those that a mesh axis runs over, the one named last changes fastest.
Arguments:
- prev_vectors: float32 [4096, 2048], P('pairs', 'vecs'), may hold values from -1 to 1
- columns: float32 [4096, 512], P('pairs'), may hold values from -20 to 200, as said below
- pivots: int32 [2, 256], replicated, may hold values from 0 to 4095, as said below
Outputs:
- new_vectors: float32 [4096, 512], P('pairs')
The draws below stay inside these ranges and needn't reach their ends.
Inputs may be any that keep to these rules, and one draw needn't show every extreme that they name: All 2 x 256 pivots are distinct. The pivots of panel c lie in the c-th of 2 equal parts of the rows of each slab of 512 pairs. A slab holds at most 64 pivots of one panel, and in every panel some slab holds exactly 64. `columns`: in every panel the residual's pivot block is symmetric positive definite.
All inputs are finite; a program needn't handle non-finite values.
Results may differ from the reference program's by a relative error of at most 0.0001.
Values sent between devices are 32-bit elements; how exact they have to be, the bound alone decides.
A program may use at most 64 MiB of HBM per device.

```python
import jax
import jax.numpy as jnp
from jax import lax

SLAB = 512
VECS = 2048
PANEL = 256
PANELS = 2
PAIRS = 4096
MOST = 64


def vector_table(key):
    subkey = jax.random.fold_in(key, 11)
    spread_scale = 0.5 ** 0.5 * VECS ** (-0.25)
    values = jnp.clip(jax.random.normal(subkey, (PAIRS, VECS), jnp.float32), -6.0, 6.0) * spread_scale
    return values


def pivot_table(key):
    slab_count = PAIRS // SLAB
    region = SLAB // PANELS
    stride = region // MOST
    tables = []
    for current in range(PANELS):
        subkey = jax.random.fold_in(key, 100 + current)
        keys = jax.random.split(subkey, 4)
        shuffle = jax.random.permutation(keys[0], slab_count * MOST).astype(jnp.int32)
        full_slab = jax.random.randint(keys[1], (), 0, slab_count)
        slot_ids = jnp.arange(slab_count * MOST, dtype=jnp.int32)
        scores = jnp.where(slot_ids // MOST == full_slab, slot_ids % MOST - MOST, shuffle)
        chosen = jnp.argsort(scores, stable=True)[:PANEL].astype(jnp.int32)
        chosen = chosen[jax.random.permutation(keys[2], PANEL)]
        owners = chosen // MOST
        within = chosen % MOST
        offsets = within * stride + jax.random.randint(keys[3], (PANEL,), 0, stride)
        tables.append(owners * SLAB + current * region + offsets)
    return jnp.stack(tables).astype(jnp.int32)


def draw_pivots(key, part):
    return pivot_table(key)


def draw_prev_vectors(key, part):
    return vector_table(key)


def draw_columns(key, part):
    pivot_all = pivot_table(key)
    vectors = vector_table(key)
    keys = jax.random.split(jax.random.fold_in(key, 23), 4)
    total_width = PANELS * PANEL
    base = jnp.clip(jax.random.normal(keys[0], (PAIRS, total_width), jnp.float32), -6.0, 6.0) * 3.0
    pivot_part = jnp.clip(jax.random.normal(keys[1], (PANELS * PANEL, total_width), jnp.float32), -6.0, 6.0) * 0.5
    base = base.at[pivot_all.reshape(-1)].set(pivot_part)
    for current in range(PANELS):
        pivot_ids = pivot_all[current]
        rows_known = vectors[pivot_ids]
        gram = jnp.dot(rows_known, rows_known.T, precision=lax.Precision.HIGHEST, preferred_element_type=jnp.float32)
        noise_key = jax.random.fold_in(keys[2], current)
        raw = jnp.clip(jax.random.normal(noise_key, (PANEL, PANEL), jnp.float32), -4.0, 4.0)
        noise = (raw + raw.T) * 0.5 ** 0.5
        diagonal = jax.random.uniform(jax.random.fold_in(keys[3], current), (PANEL,), jnp.float32, 72.0, 128.0)
        block = gram + noise + jnp.diag(diagonal) + 1.0
        column_ids = current * PANEL + jnp.arange(PANEL, dtype=jnp.int32)
        base = base.at[pivot_ids[:, None], column_ids[None, :]].set(block)
    return base


def setup_inputs(seed: int = 0) -> dict:
    key_list = jax.random.split(jax.random.key(seed), 4)
    return {
        "prev_vectors": draw_prev_vectors(jax.random.fold_in(key_list[3], 71), 0),
        "columns": draw_columns(jax.random.fold_in(key_list[3], 71), 0),
        "pivots": draw_pivots(jax.random.fold_in(key_list[3], 71), 0),
    }


def product(left, right):
    return jnp.dot(left.astype(jnp.float32), right.T.astype(jnp.float32), precision=lax.Precision.HIGHEST, preferred_element_type=jnp.float32)

def reference(prev_vectors, columns, pivots):
    blocks = []
    for current in range(PANELS):
        pivot_ids = pivots[current].astype(jnp.int32)
        products = product(prev_vectors, prev_vectors[pivot_ids])
        for block in blocks:
            products = products + product(block, block[pivot_ids])
        panel_columns = columns[:, current * PANEL:(current + 1) * PANEL]
        residual = panel_columns - products
        pivot_block = residual[pivot_ids]
        symmetric = 0.5 * (pivot_block + pivot_block.T)
        factor = jnp.linalg.cholesky(symmetric)
        solved = jax.scipy.linalg.solve_triangular(factor, residual.T, lower=True)
        blocks.append(solved.T)
    return jnp.concatenate(blocks, axis=1)
```

```python
import functools

import jax
import jax.numpy as jnp
from jax import lax
from jax.experimental import pallas as pl
from jax.experimental.pallas import tpu as pltpu
from jax.sharding import PartitionSpec as P

F32 = jnp.float32
BF16 = jnp.bfloat16
STEP = 16


def split2(x):
    high = x.astype(BF16)
    return high, (x - high.astype(F32)).astype(BF16)


def split3(x):
    high = x.astype(BF16)
    rest = x - high.astype(F32)
    mid = rest.astype(BF16)
    return high, mid, (rest - mid.astype(F32)).astype(BF16)


def dot(a, b, dims):
    return lax.dot_general(a, b, (dims, ((), ())), preferred_element_type=F32)


def dot_nt(a, b):
    nt = ((1,), (1,))
    return dot(a[0], b[0], nt) + (dot(a[0], b[1], nt) + dot(a[1], b[0], nt))


def eliminate(work, inverse, chunk, chunks):
    size = work.shape[0]
    per = size // chunks
    first = chunk * per
    lane0 = first // 128 * 128
    lane1 = size + -(-(first + per) // 128) * 128
    row_ids = lax.broadcasted_iota(jnp.int32, (STEP, 128), 0)

    def group(g, _):
        row = pl.multiple_of(g * STEP, STEP)
        band = work[pl.ds(row, STEP), lane0:lane1]
        shift = lax.rem(128 - lax.rem(row, 128), 128)
        near = pltpu.roll(band[:, :128], shift, 1)
        cols = [jnp.broadcast_to(near[:, j : j + 1], (STEP, 128)) for j in range(STEP)]
        tiles = [band[:, t : t + 128] for t in range(0, lane1 - lane0, 128)]
        diag = jnp.ones((STEP, 128), F32)
        for k in range(STEP):
            pivot = cols[k][k : k + 1, :]
            diag = jnp.where(row_ids == k, pivot, diag)
            if k == STEP - 1:
                break
            mult = jnp.where(row_ids > k, cols[k] * (1.0 / pivot), 0.0)
            for j in range(k + 1, STEP):
                cols[j] = cols[j] - mult * cols[j][k : k + 1, :]
            tiles = [t - mult * t[k : k + 1, :] for t in tiles]
        scale = lax.rsqrt(diag)
        band = jnp.concatenate([t * scale for t in tiles], axis=1)
        inverse[pl.ds(row, STEP), : lane1 - size] = band[:, size - lane0 :]
        h, m, l = split3(band)
        left = jnp.concatenate([h, h, m, h, l, m], axis=0)[:, first - lane0 : size - lane0]
        right = jnp.concatenate([h, m, h, l, h, m], axis=0)
        work[first:, lane0:lane1] = work[first:, lane0:lane1] - dot(left, right, ((0,), (0,)))
        return 0

    lax.fori_loop(first // STEP, (first + per) // STEP, group, 0)


def set_work(work, inverse, symmetric):
    size = symmetric.shape[0]
    rows = lax.broadcasted_iota(jnp.int32, (size, size), 0)
    lanes = lax.broadcasted_iota(jnp.int32, (size, size), 1)
    work[:, :size] = symmetric
    work[:, size:] = jnp.where(rows == lanes, 1.0, 0.0).astype(F32)
    inverse[...] = jnp.zeros_like(inverse)


def kernel(
    pair_count, sent_ref, pos_ref, prev_ref, cols_ref, out_ref,
    table, p_high, p_low,
    x1, a1, b1, f1, x2, a2, b2, f2, x3, a3, b3, f3,
    work1, inv1, work2, inv2,
    z_send, z_recv, x_send, x_recv, r_send, r_recv,
):
    panels, slots, _ = sent_ref.shape
    depth = prev_ref.shape[1]
    width = cols_ref.shape[1] // panels
    outer = pair_count // 2
    me = lax.axis_index("pairs")
    vec = lax.axis_index("vecs")
    zi, xi = me // 2, lax.rem(me, 2)
    vy, vc = vec // 2, lax.rem(vec, 2)
    x_peer = {"pairs": zi * 2 + 1 - xi}
    c_peer = {"vecs": vy * 2 + 1 - vc}
    y_peer = {"vecs": (1 - vy) * 2 + vc}
    z_peers = [{"pairs": lax.rem(zi + d, outer) * 2 + xi} for d in range(1, outer)]
    mesh_id = pl.DeviceIdType.MESH

    barrier = pltpu.get_barrier_semaphore()
    everyone = [x_peer, c_peer, y_peer] + z_peers
    for peer in everyone:
        pl.semaphore_signal(barrier, inc=1, device_id=peer, device_id_type=mesh_id)
    pl.semaphore_wait(barrier, len(everyone))

    def rows_of(z, x):
        return pl.ds(pl.multiple_of((z * 2 + x) * slots, slots), slots)

    def z_copy(c, d):
        return pltpu.make_async_remote_copy(
            src_ref=sent_ref.at[c], dst_ref=table.at[c, rows_of(zi, xi)],
            send_sem=z_send.at[c, d], recv_sem=z_recv.at[c, d],
            device_id=z_peers[d - 1], device_id_type=mesh_id,
        )

    def z_arrival(c, d):
        return pltpu.make_async_remote_copy(
            src_ref=sent_ref.at[c], dst_ref=table.at[c, rows_of(lax.rem(zi + outer - d, outer), xi)],
            send_sem=z_send.at[c, d], recv_sem=z_recv.at[c, d],
            device_id=z_peers[d - 1], device_id_type=mesh_id,
        )

    def x_copy(c, d):
        rows = rows_of(lax.rem(zi + outer - d, outer), xi)
        return pltpu.make_async_remote_copy(
            src_ref=sent_ref.at[c] if d == 0 else table.at[c, rows], dst_ref=table.at[c, rows],
            send_sem=x_send.at[c, d], recv_sem=x_recv.at[c, d],
            device_id=x_peer, device_id_type=mesh_id,
        )

    def x_arrival(c, d):
        rows = rows_of(lax.rem(zi + outer - d, outer), 1 - xi)
        return pltpu.make_async_remote_copy(
            src_ref=sent_ref.at[c], dst_ref=table.at[c, rows],
            send_sem=x_send.at[c, d], recv_sem=x_recv.at[c, d],
            device_id=x_peer, device_id_type=mesh_id,
        )

    def forward(c):
        for d in range(1, outer):
            z_arrival(c, d).wait_recv()
            x_copy(c, d).start()

    def finish_gather(c):
        for d in range(outer):
            x_arrival(c, d).wait_recv()

    def half(ref, which):
        count = ref.shape[0] // 2
        return ref.at[pl.ds(pl.multiple_of(which * count, count), count)]

    def exchange(src, dst, n, stage, peer):
        return pltpu.make_async_remote_copy(
            src_ref=src, dst_ref=dst, send_sem=r_send.at[n, stage], recv_sem=r_recv.at[n, stage],
            device_id=peer, device_id_type=mesh_id,
        )

    def stage_a(n, x, a):
        return exchange(half(x, 1 - vc), a, n, 0, c_peer)

    def stage_b(n, x, b):
        return exchange(half(x, vc), b, n, 1, y_peer)

    def stage_c(n, f):
        return exchange(half(f, vc), half(f, vc), n, 2, c_peer)

    def stage_c_arrival(n, f):
        return exchange(half(f, 1 - vc), half(f, 1 - vc), n, 2, c_peer)

    def a_to_b(n, x, a, b):
        stage_a(n, x, a).wait_recv()
        own = half(x, vc)
        own[...] = own[...] + a[...]
        stage_b(n, x, b).start()

    def b_to_c(n, x, b, f):
        stage_b(n, x, b).wait_recv()
        half(f, vc)[...] = half(x, vc)[...] + b[...]
        stage_c(n, f).start()

    for c in range(panels):
        for d in range(1, outer):
            z_copy(c, d).start()
        if c == 0:
            x_copy(c, 0).start()
    for c in range(1, panels):
        x_copy(c, 0).start()
    for c in range(panels):
        table[c, rows_of(zi, xi)] = sent_ref[c]

    quarter = cols_ref.shape[1] // 4

    def ordered(c):
        place = pos_ref[c]
        count = pair_count * slots
        hit = lax.broadcasted_iota(jnp.int32, (width, count), 1) == place
        pick = jnp.where(hit, 1.0, 0.0).astype(BF16)
        nn = ((1,), (0,))
        high, low = split2(table[c, :, :depth])
        p_high[c] = dot(pick, high, nn).astype(BF16)
        p_low[c] = dot(pick, low, nn).astype(BF16)
        th, tm, tl = split3(table[c, :, depth:])
        return dot(pick, th, nn) + dot(pick, tm, nn) + dot(pick, tl, nn)

    def place_share(share, lanes):
        tiles = []
        for q in range(lanes // quarter):
            tiles.append(jnp.where(vec == q, share, 0.0))
        return jnp.concatenate(tiles, axis=1)

    forward(0)
    finish_gather(0)
    share = ordered(0)
    rows0 = (p_high[0], p_low[0])
    x1[...] = place_share(share, width) - dot_nt(rows0, rows0)
    stage_a(0, x1, a1).start()
    a_to_b(0, x1, a1, b1)
    forward(1)
    b_to_c(0, x1, b1, f1)
    stage_c_arrival(0, f1).wait_recv()

    block = f1[...]
    set_work(work1, inv1, 0.5 * (block + block.T))
    eliminate(work1, inv1, 0, 4)

    finish_gather(1)
    share = ordered(1)
    rows0 = (p_high[0], p_low[0])
    rows1 = (p_high[1], p_low[1])
    known = jnp.concatenate([dot_nt(rows1, rows0), dot_nt(rows1, rows1)], axis=1)
    x2[...] = place_share(share, 2 * width) - known
    stage_a(1, x2, a2).start()
    own = split2(prev_ref[...])
    x3[:, :width] = dot_nt(own, rows0)
    x3[:, width:] = dot_nt(own, rows1)
    stage_a(2, x3, a3).start()
    a_to_b(1, x2, a2, b2)
    eliminate(work1, inv1, 1, 4)
    a_to_b(2, x3, a3, b3)
    eliminate(work1, inv1, 2, 4)
    b_to_c(1, x2, b2, f2)
    eliminate(work1, inv1, 3, 4)
    stage_c_arrival(1, f2).wait_recv()

    inverse1 = split2(inv1[...])
    cross = split2(dot_nt(split2(f2[:, :width]), inverse1))
    block = f2[:, width:] - dot_nt(cross, cross)
    set_work(work2, inv2, 0.5 * (block + block.T))
    eliminate(work2, inv2, 0, 4)
    eliminate(work2, inv2, 1, 4)
    b_to_c(2, x3, b3, f3)
    eliminate(work2, inv2, 2, 4)
    stage_c_arrival(2, f3).wait_recv()
    new1 = dot_nt(split2(cols_ref[:, :width] - f3[:, :width]), inverse1)
    out_ref[:, :width] = new1
    rest = cols_ref[:, width:] - f3[:, width:] - dot_nt(split2(new1), cross)
    eliminate(work2, inv2, 3, 4)
    out_ref[:, width:] = dot_nt(split2(rest), split2(inv2[...]))

    for c in range(panels):
        for d in range(1, outer):
            z_copy(c, d).wait_send()
        for d in range(outer):
            x_copy(c, d).wait_send()
    for n, (x, a, b, f) in enumerate(((x1, a1, b1, f1), (x2, a2, b2, f2), (x3, a3, b3, f3))):
        stage_a(n, x, a).wait_send()
        stage_b(n, x, b).wait_send()
        stage_c(n, f).wait_send()


def body(prev_vectors, columns, pivots):
    slab_rows, depth = prev_vectors.shape
    panels, width = pivots.shape
    pair_count = lax.axis_size("pairs")
    slots = max(8, 2 * width // pair_count)
    me = lax.axis_index("pairs")
    vec = lax.axis_index("vecs")
    owners = pivots // slab_rows
    order = jnp.arange(width, dtype=jnp.int32)
    earlier = (owners[:, :, None] == owners[:, None, :]) & (order[None, None, :] < order[None, :, None])
    rank = jnp.sum(earlier.astype(jnp.int32), axis=2)
    place = owners * slots + rank
    wanted = me * slots + jnp.arange(slots, dtype=jnp.int32)
    hit = place[:, None, :] == wanted[None, :, None]
    local = jnp.sum(jnp.where(hit, (pivots - me * slab_rows)[:, None, :], 0), axis=2).reshape(-1)
    quarter = columns.shape[1] // lax.axis_size("vecs")
    share = lax.dynamic_slice_in_dim(columns, vec * quarter, quarter, 1)
    sent = jnp.concatenate([prev_vectors[local], share[local]], axis=1)
    sent = sent.reshape(panels, slots, depth + quarter)
    count = pair_count * slots
    outer = pair_count // 2

    def vmem(*shape, dtype=F32):
        return pltpu.VMEM(shape, dtype)

    def reduced(rows, lanes):
        return [vmem(rows, lanes), vmem(rows // 2, lanes), vmem(rows // 2, lanes), vmem(rows, lanes)]

    scratch = [
        vmem(panels, count, depth + quarter),
        vmem(panels, width, depth, dtype=BF16),
        vmem(panels, width, depth, dtype=BF16),
        *reduced(width, width),
        *reduced(width, 2 * width),
        *reduced(slab_rows, 2 * width),
        vmem(width, 2 * width), vmem(width, width),
        vmem(width, 2 * width), vmem(width, width),
        pltpu.SemaphoreType.DMA((panels, outer)),
        pltpu.SemaphoreType.DMA((panels, outer)),
        pltpu.SemaphoreType.DMA((panels, outer)),
        pltpu.SemaphoreType.DMA((panels, outer)),
        pltpu.SemaphoreType.DMA((3, 3)),
        pltpu.SemaphoreType.DMA((3, 3)),
    ]
    whole = pl.BlockSpec(memory_space=pltpu.VMEM)
    return pl.pallas_call(
        functools.partial(kernel, pair_count),
        out_shape=jax.ShapeDtypeStruct((slab_rows, panels * width), F32),
        in_specs=[whole] * 4,
        out_specs=whole,
        scratch_shapes=scratch,
        compiler_params=pltpu.CompilerParams(
            collective_id=0, has_side_effects=True, vmem_limit_bytes=48 * 1024 * 1024
        ),
    )(sent, place[:, :, None], prev_vectors, columns)


def solution(mesh):
    placed = (P("pairs", "vecs"), P("pairs", None), P())
    return jax.shard_map(
        body, mesh=mesh, in_specs=placed, out_specs=P("pairs", None), check_vma=False
    )
```

```python
import functools

import jax
import jax.numpy as jnp
from jax import lax
from jax.experimental import pallas as pl
from jax.experimental.pallas import tpu as pltpu
from jax.sharding import PartitionSpec as P

F32 = jnp.float32
BF16 = jnp.bfloat16
STEP = 16


def split2(x):
    high = x.astype(BF16)
    return high, (x - high.astype(F32)).astype(BF16)


def split3(x):
    high = x.astype(BF16)
    rest = x - high.astype(F32)
    mid = rest.astype(BF16)
    return high, mid, (rest - mid.astype(F32)).astype(BF16)


def dot(a, b, dims):
    return lax.dot_general(a, b, (dims, ((), ())), preferred_element_type=F32)


def dot_nt(a, b):
    nt = ((1,), (1,))
    return dot(a[0], b[0], nt) + (dot(a[0], b[1], nt) + dot(a[1], b[0], nt))


def live_tiles(size, row):
    return range(row // 128, size // 128 + row // 128 + 1)


def start_band(work):
    return {t: work[:STEP, t * 128 : t * 128 + 128] for t in live_tiles(work.shape[0], 0)}


def eliminate(work, inverse, chunk, chunks, band):
    size = work.shape[0]
    parts = size // 128
    per = size // STEP // chunks
    row_ids = lax.broadcasted_iota(jnp.int32, (STEP, 128), 0)
    for g in range(chunk * per, (chunk + 1) * per):
        row = g * STEP
        lane = row % 128
        names = live_tiles(size, row)
        tiles = [band[t] for t in names]
        cols = [jnp.broadcast_to(tiles[0][:, lane + j : lane + j + 1], (STEP, 128)) for j in range(STEP)]
        diag = jnp.ones((STEP, 128), F32)
        for k in range(STEP):
            pivot = cols[k][k : k + 1, :]
            diag = jnp.where(row_ids == k, pivot, diag)
            if k == STEP - 1:
                break
            mult = jnp.where(row_ids > k, cols[k] * (1.0 / pivot), 0.0)
            for j in range(k + 1, STEP):
                cols[j] = cols[j] - mult * cols[j][k : k + 1, :]
            tiles = [t - mult * t[k : k + 1, :] for t in tiles]
        scale = lax.rsqrt(diag)
        tiles = [t * scale for t in tiles]
        for t, tile in zip(names, tiles):
            if t >= parts:
                inverse[row : row + STEP, (t - parts) * 128 : (t - parts) * 128 + 128] = tile
        after = row + STEP
        if after == size:
            return None
        lane0 = names[0] * 128
        lane1 = lane0 + 128 * len(tiles)
        h, m, l = split3(jnp.concatenate(tiles, axis=1))
        left = jnp.concatenate([h, h, m, h, l, m], axis=0)
        right = jnp.concatenate([h, m, h, l, h, m], axis=0)
        near = dot(left[:, after - lane0 : after + STEP - lane0], right, ((0,), (0,)))
        band = {}
        for t in live_tiles(size, after):
            band[t] = work[after : after + STEP, t * 128 : t * 128 + 128]
            if t in names:
                band[t] = band[t] - near[:, t * 128 - lane0 : t * 128 - lane0 + 128]
        rest = after + STEP
        if rest < size:
            far = dot(left[:, rest - lane0 : size - lane0], right, ((0,), (0,)))
            work[rest:, lane0:lane1] = work[rest:, lane0:lane1] - far
    return band


def set_work(work, inverse, symmetric):
    size = symmetric.shape[0]
    rows = lax.broadcasted_iota(jnp.int32, (size, size), 0)
    lanes = lax.broadcasted_iota(jnp.int32, (size, size), 1)
    work[:, :size] = symmetric
    work[:, size:] = jnp.where(rows == lanes, 1.0, 0.0).astype(F32)
    inverse[...] = jnp.zeros_like(inverse)


def kernel(
    pair_count, sent_ref, pos_ref, prev_ref, cols_ref, out_ref,
    table, p_high, p_low,
    x1, a1, b1, f1, x2, a2, b2, f2, x3, a3, b3, f3,
    work1, inv1, work2, inv2,
    z_send, z_recv, x_send, x_recv, r_send, r_recv,
):
    panels, slots, _ = sent_ref.shape
    depth = prev_ref.shape[1]
    width = cols_ref.shape[1] // panels
    outer = pair_count // 2
    me = lax.axis_index("pairs")
    vec = lax.axis_index("vecs")
    zi, xi = me // 2, lax.rem(me, 2)
    vy, vc = vec // 2, lax.rem(vec, 2)
    x_peer = {"pairs": zi * 2 + 1 - xi}
    c_peer = {"vecs": vy * 2 + 1 - vc}
    y_peer = {"vecs": (1 - vy) * 2 + vc}
    z_peers = [{"pairs": lax.rem(zi + d, outer) * 2 + xi} for d in range(1, outer)]
    mesh_id = pl.DeviceIdType.MESH

    barrier = pltpu.get_barrier_semaphore()
    everyone = [x_peer, c_peer, y_peer] + z_peers
    for peer in everyone:
        pl.semaphore_signal(barrier, inc=1, device_id=peer, device_id_type=mesh_id)
    pl.semaphore_wait(barrier, len(everyone))

    def rows_of(z, x):
        return pl.ds(pl.multiple_of((z * 2 + x) * slots, slots), slots)

    def z_copy(c, d):
        return pltpu.make_async_remote_copy(
            src_ref=sent_ref.at[c], dst_ref=table.at[c, rows_of(zi, xi)],
            send_sem=z_send.at[c, d], recv_sem=z_recv.at[c, d],
            device_id=z_peers[d - 1], device_id_type=mesh_id,
        )

    def z_arrival(c, d):
        return pltpu.make_async_remote_copy(
            src_ref=sent_ref.at[c], dst_ref=table.at[c, rows_of(lax.rem(zi + outer - d, outer), xi)],
            send_sem=z_send.at[c, d], recv_sem=z_recv.at[c, d],
            device_id=z_peers[d - 1], device_id_type=mesh_id,
        )

    def x_copy(c, d):
        rows = rows_of(lax.rem(zi + outer - d, outer), xi)
        return pltpu.make_async_remote_copy(
            src_ref=sent_ref.at[c] if d == 0 else table.at[c, rows], dst_ref=table.at[c, rows],
            send_sem=x_send.at[c, d], recv_sem=x_recv.at[c, d],
            device_id=x_peer, device_id_type=mesh_id,
        )

    def x_arrival(c, d):
        rows = rows_of(lax.rem(zi + outer - d, outer), 1 - xi)
        return pltpu.make_async_remote_copy(
            src_ref=sent_ref.at[c], dst_ref=table.at[c, rows],
            send_sem=x_send.at[c, d], recv_sem=x_recv.at[c, d],
            device_id=x_peer, device_id_type=mesh_id,
        )

    def forward(c):
        for d in range(1, outer):
            z_arrival(c, d).wait_recv()
            x_copy(c, d).start()

    def finish_gather(c):
        for d in range(outer):
            x_arrival(c, d).wait_recv()

    def half(ref, which):
        count = ref.shape[0] // 2
        return ref.at[pl.ds(pl.multiple_of(which * count, count), count)]

    def exchange(src, dst, n, stage, peer):
        return pltpu.make_async_remote_copy(
            src_ref=src, dst_ref=dst, send_sem=r_send.at[n, stage], recv_sem=r_recv.at[n, stage],
            device_id=peer, device_id_type=mesh_id,
        )

    def stage_a(n, x, a):
        return exchange(half(x, 1 - vc), a, n, 0, c_peer)

    def stage_b(n, x, b):
        return exchange(half(x, vc), b, n, 1, y_peer)

    def stage_c(n, f):
        return exchange(half(f, vc), half(f, vc), n, 2, c_peer)

    def stage_c_arrival(n, f):
        return exchange(half(f, 1 - vc), half(f, 1 - vc), n, 2, c_peer)

    def a_to_b(n, x, a, b):
        stage_a(n, x, a).wait_recv()
        own = half(x, vc)
        own[...] = own[...] + a[...]
        stage_b(n, x, b).start()

    def b_to_c(n, x, b, f):
        stage_b(n, x, b).wait_recv()
        half(f, vc)[...] = half(x, vc)[...] + b[...]
        stage_c(n, f).start()

    def begin(c):
        for d in range(1, outer):
            z_copy(c, d).start()
        x_copy(c, 0).start()

    begin(0)
    for c in range(panels):
        table[c, rows_of(zi, xi)] = sent_ref[c]

    quarter = cols_ref.shape[1] // 4

    def ordered(c):
        place = pos_ref[c]
        count = pair_count * slots
        hit = lax.broadcasted_iota(jnp.int32, (width, count), 1) == place
        pick = jnp.where(hit, 1.0, 0.0).astype(BF16)
        nn = ((1,), (0,))
        high, low = split2(table[c, :, :depth])
        p_high[c] = dot(pick, high, nn).astype(BF16)
        p_low[c] = dot(pick, low, nn).astype(BF16)
        th, tm, tl = split3(table[c, :, depth:])
        return dot(pick, th, nn) + dot(pick, tm, nn) + dot(pick, tl, nn)

    def place_share(share, lanes):
        tiles = []
        for q in range(lanes // quarter):
            tiles.append(jnp.where(vec == q, share, 0.0))
        return jnp.concatenate(tiles, axis=1)

    forward(0)
    begin(1)
    finish_gather(0)
    share = ordered(0)
    rows0 = (p_high[0], p_low[0])
    x1[...] = place_share(share, width) - dot_nt(rows0, rows0)
    stage_a(0, x1, a1).start()
    a_to_b(0, x1, a1, b1)
    forward(1)
    b_to_c(0, x1, b1, f1)
    stage_c_arrival(0, f1).wait_recv()

    block = f1[...]
    set_work(work1, inv1, 0.5 * (block + block.T))
    band = eliminate(work1, inv1, 0, 4, start_band(work1))

    finish_gather(1)
    share = ordered(1)
    rows0 = (p_high[0], p_low[0])
    rows1 = (p_high[1], p_low[1])
    known = jnp.concatenate([dot_nt(rows1, rows0), dot_nt(rows1, rows1)], axis=1)
    x2[...] = place_share(share, 2 * width) - known
    stage_a(1, x2, a2).start()
    own = split2(prev_ref[...])
    x3[:, :width] = dot_nt(own, rows0)
    x3[:, width:] = dot_nt(own, rows1)
    stage_a(2, x3, a3).start()
    a_to_b(1, x2, a2, b2)
    band = eliminate(work1, inv1, 1, 4, band)
    a_to_b(2, x3, a3, b3)
    band = eliminate(work1, inv1, 2, 4, band)
    b_to_c(1, x2, b2, f2)
    band = eliminate(work1, inv1, 3, 4, band)
    stage_c_arrival(1, f2).wait_recv()

    inverse1 = split2(inv1[...])
    cross = split2(dot_nt(split2(f2[:, :width]), inverse1))
    block = f2[:, width:] - dot_nt(cross, cross)
    set_work(work2, inv2, 0.5 * (block + block.T))
    band = eliminate(work2, inv2, 0, 4, start_band(work2))
    band = eliminate(work2, inv2, 1, 4, band)
    b_to_c(2, x3, b3, f3)
    band = eliminate(work2, inv2, 2, 4, band)
    stage_c_arrival(2, f3).wait_recv()
    new1 = dot_nt(split2(cols_ref[:, :width] - f3[:, :width]), inverse1)
    out_ref[:, :width] = new1
    rest = cols_ref[:, width:] - f3[:, width:] - dot_nt(split2(new1), cross)
    band = eliminate(work2, inv2, 3, 4, band)
    out_ref[:, width:] = dot_nt(split2(rest), split2(inv2[...]))

    for c in range(panels):
        for d in range(1, outer):
            z_copy(c, d).wait_send()
        for d in range(outer):
            x_copy(c, d).wait_send()
    for n, (x, a, b, f) in enumerate(((x1, a1, b1, f1), (x2, a2, b2, f2), (x3, a3, b3, f3))):
        stage_a(n, x, a).wait_send()
        stage_b(n, x, b).wait_send()
        stage_c(n, f).wait_send()


def body(prev_vectors, columns, pivots):
    slab_rows, depth = prev_vectors.shape
    panels, width = pivots.shape
    pair_count = lax.axis_size("pairs")
    slots = max(8, 2 * width // pair_count)
    me = lax.axis_index("pairs")
    vec = lax.axis_index("vecs")
    owners = lax.div(pivots, jnp.int32(slab_rows))
    order = jnp.arange(width, dtype=jnp.int32)
    earlier = (owners[:, :, None] == owners[:, None, :]) & (order[None, None, :] < order[None, :, None])
    rank = jnp.sum(earlier.astype(jnp.int32), axis=2)
    place = owners * slots + rank
    wanted = me * slots + jnp.arange(slots, dtype=jnp.int32)
    hit = place[:, None, :] == wanted[None, :, None]
    local = jnp.sum(jnp.where(hit, (pivots - me * slab_rows)[:, None, :], 0), axis=2).reshape(-1)
    quarter = columns.shape[1] // lax.axis_size("vecs")
    share = lax.dynamic_slice_in_dim(columns[local], vec * quarter, quarter, 1)
    sent = jnp.concatenate([prev_vectors[local], share], axis=1)
    sent = sent.reshape(panels, slots, depth + quarter)
    count = pair_count * slots
    outer = pair_count // 2

    def vmem(*shape, dtype=F32):
        return pltpu.VMEM(shape, dtype)

    def reduced(rows, lanes):
        return [vmem(rows, lanes), vmem(rows // 2, lanes), vmem(rows // 2, lanes), vmem(rows, lanes)]

    scratch = [
        vmem(panels, count, depth + quarter),
        vmem(panels, width, depth, dtype=BF16),
        vmem(panels, width, depth, dtype=BF16),
        *reduced(width, width),
        *reduced(width, 2 * width),
        *reduced(slab_rows, 2 * width),
        vmem(width, 2 * width), vmem(width, width),
        vmem(width, 2 * width), vmem(width, width),
        pltpu.SemaphoreType.DMA((panels, outer)),
        pltpu.SemaphoreType.DMA((panels, outer)),
        pltpu.SemaphoreType.DMA((panels, outer)),
        pltpu.SemaphoreType.DMA((panels, outer)),
        pltpu.SemaphoreType.DMA((3, 3)),
        pltpu.SemaphoreType.DMA((3, 3)),
    ]
    whole = pl.BlockSpec(memory_space=pltpu.VMEM)
    return pl.pallas_call(
        functools.partial(kernel, pair_count),
        out_shape=jax.ShapeDtypeStruct((slab_rows, panels * width), F32),
        in_specs=[whole] * 4,
        out_specs=whole,
        scratch_shapes=scratch,
        compiler_params=pltpu.CompilerParams(
            collective_id=0, has_side_effects=True, vmem_limit_bytes=48 * 1024 * 1024
        ),
    )(sent, place[:, :, None], prev_vectors, columns)


def solution(mesh):
    placed = (P("pairs", "vecs"), P("pairs", None), P())
    return jax.shard_map(
        body, mesh=mesh, in_specs=placed, out_specs=P("pairs", None), check_vma=False
    )
```

```python
import functools

import jax
import jax.numpy as jnp
from jax import lax
from jax.experimental import pallas as pl
from jax.experimental.pallas import tpu as pltpu
from jax.sharding import PartitionSpec as P

F32 = jnp.float32
BF16 = jnp.bfloat16
STEP = 16


def split2(x):
    high = x.astype(BF16)
    return high, (x - high.astype(F32)).astype(BF16)


def split3(x):
    high = x.astype(BF16)
    rest = x - high.astype(F32)
    mid = rest.astype(BF16)
    return high, mid, (rest - mid.astype(F32)).astype(BF16)


def dot(a, b, dims):
    return lax.dot_general(a, b, (dims, ((), ())), preferred_element_type=F32)


def dot_nt(a, b):
    nt = ((1,), (1,))
    return dot(a[0], b[0], nt) + (dot(a[0], b[1], nt) + dot(a[1], b[0], nt))


def live_tiles(size, row):
    return range(row // 128, size // 128 + row // 128 + 1)


def start_band(work):
    return {t: work[:STEP, t * 128 : t * 128 + 128] for t in live_tiles(work.shape[0], 0)}


def inverse_of(x):
    guess = pl.reciprocal(x, approx=True)
    guess = guess * (2.0 - x * guess)
    return guess * (2.0 - x * guess)


def eliminate(work, inverse, chunk, chunks, band):
    size = work.shape[0]
    parts = size // 128
    per = size // STEP // chunks
    row_ids = lax.broadcasted_iota(jnp.int32, (STEP, 128), 0)
    for g in range(chunk * per, (chunk + 1) * per):
        row = g * STEP
        lane = row % 128
        names = live_tiles(size, row)
        tiles = [band[t] for t in names]
        cols = [jnp.broadcast_to(tiles[0][:, lane + j : lane + j + 1], (STEP, 128)) for j in range(STEP)]
        diag = jnp.ones((STEP, 128), F32)
        for k in range(0, STEP, 2):
            p, q = cols[k], cols[k + 1]
            a, b, c = p[k : k + 1, :], p[k + 1 : k + 2, :], q[k + 1 : k + 2, :]
            over_a = inverse_of(a)
            over_det = inverse_of(a * c - b * b)
            ratio = b * over_a
            diag = jnp.where(row_ids == k, a, jnp.where(row_ids == k + 1, c - b * ratio, diag))
            first_mult = jnp.where(row_ids > k + 1, p * over_a, 0.0)
            second_mult = jnp.where(row_ids > k + 1, (q - ratio * p) * (a * over_det), 0.0)
            pair_mult = jnp.where(row_ids == k + 1, ratio, first_mult)

            def step(x):
                top = x[k : k + 1, :]
                low = x[k + 1 : k + 2, :] - ratio * top
                return x - pair_mult * top - second_mult * low

            for j in range(k + 2, STEP):
                cols[j] = step(cols[j])
            tiles = [step(t) for t in tiles]
        scale = lax.rsqrt(diag)
        tiles = [t * scale for t in tiles]
        for t, tile in zip(names, tiles):
            if t >= parts:
                inverse[row : row + STEP, (t - parts) * 128 : (t - parts) * 128 + 128] = tile
        after = row + STEP
        if after == size:
            return None
        lane0 = names[0] * 128
        lane1 = lane0 + 128 * len(tiles)
        h, m, l = split3(jnp.concatenate(tiles, axis=1))
        left = jnp.concatenate([h, h, m, h, l, m], axis=0)
        right = jnp.concatenate([h, m, h, l, h, m], axis=0)
        near = dot(left[:, after - lane0 : after + STEP - lane0], right, ((0,), (0,)))
        band = {}
        for t in live_tiles(size, after):
            band[t] = work[after : after + STEP, t * 128 : t * 128 + 128]
            if t in names:
                band[t] = band[t] - near[:, t * 128 - lane0 : t * 128 - lane0 + 128]
        rest = after + STEP
        if rest < size:
            far = dot(left[:, rest - lane0 : size - lane0], right, ((0,), (0,)))
            work[rest:, lane0:lane1] = work[rest:, lane0:lane1] - far
    return band


def set_work(work, inverse, symmetric):
    size = symmetric.shape[0]
    rows = lax.broadcasted_iota(jnp.int32, (size, size), 0)
    lanes = lax.broadcasted_iota(jnp.int32, (size, size), 1)
    diagonal = jnp.where(rows == lanes, symmetric, 0.0)
    down = lax.rsqrt(jnp.sum(diagonal, axis=1, keepdims=True))
    along = lax.rsqrt(jnp.sum(diagonal, axis=0, keepdims=True))
    work[:, :size] = symmetric * down * along
    work[:, size:] = jnp.where(rows == lanes, down, 0.0)
    inverse[...] = jnp.zeros_like(inverse)


def kernel(
    pair_count, sent_ref, pos_ref, prev_ref, cols_ref, out_ref,
    table, p_high, p_low,
    x1, a1, b1, f1, x2, a2, b2, f2, x3, a3, b3, f3,
    work1, inv1, work2, inv2,
    z_send, z_recv, x_send, x_recv, r_send, r_recv,
):
    panels, slots, _ = sent_ref.shape
    depth = prev_ref.shape[1]
    width = cols_ref.shape[1] // panels
    outer = pair_count // 2
    me = lax.axis_index("pairs")
    vec = lax.axis_index("vecs")
    zi, xi = me // 2, lax.rem(me, 2)
    vy, vc = vec // 2, lax.rem(vec, 2)
    x_peer = {"pairs": zi * 2 + 1 - xi}
    c_peer = {"vecs": vy * 2 + 1 - vc}
    y_peer = {"vecs": (1 - vy) * 2 + vc}
    z_peers = [{"pairs": lax.rem(zi + d, outer) * 2 + xi} for d in range(1, outer)]
    mesh_id = pl.DeviceIdType.MESH

    barrier = pltpu.get_barrier_semaphore()
    everyone = [x_peer, c_peer, y_peer] + z_peers
    for peer in everyone:
        pl.semaphore_signal(barrier, inc=1, device_id=peer, device_id_type=mesh_id)
    pl.semaphore_wait(barrier, len(everyone))

    def rows_of(z, x):
        return pl.ds(pl.multiple_of((z * 2 + x) * slots, slots), slots)

    def z_copy(c, d):
        return pltpu.make_async_remote_copy(
            src_ref=sent_ref.at[c], dst_ref=table.at[c, rows_of(zi, xi)],
            send_sem=z_send.at[c, d], recv_sem=z_recv.at[c, d],
            device_id=z_peers[d - 1], device_id_type=mesh_id,
        )

    def z_arrival(c, d):
        return pltpu.make_async_remote_copy(
            src_ref=sent_ref.at[c], dst_ref=table.at[c, rows_of(lax.rem(zi + outer - d, outer), xi)],
            send_sem=z_send.at[c, d], recv_sem=z_recv.at[c, d],
            device_id=z_peers[d - 1], device_id_type=mesh_id,
        )

    def x_copy(c, d):
        rows = rows_of(lax.rem(zi + outer - d, outer), xi)
        return pltpu.make_async_remote_copy(
            src_ref=sent_ref.at[c] if d == 0 else table.at[c, rows], dst_ref=table.at[c, rows],
            send_sem=x_send.at[c, d], recv_sem=x_recv.at[c, d],
            device_id=x_peer, device_id_type=mesh_id,
        )

    def x_arrival(c, d):
        rows = rows_of(lax.rem(zi + outer - d, outer), 1 - xi)
        return pltpu.make_async_remote_copy(
            src_ref=sent_ref.at[c], dst_ref=table.at[c, rows],
            send_sem=x_send.at[c, d], recv_sem=x_recv.at[c, d],
            device_id=x_peer, device_id_type=mesh_id,
        )

    def forward(c):
        for d in range(1, outer):
            z_arrival(c, d).wait_recv()
            x_copy(c, d).start()

    def finish_gather(c):
        for d in range(outer):
            x_arrival(c, d).wait_recv()

    def half(ref, which):
        count = ref.shape[0] // 2
        return ref.at[pl.ds(pl.multiple_of(which * count, count), count)]

    def exchange(src, dst, n, stage, peer):
        return pltpu.make_async_remote_copy(
            src_ref=src, dst_ref=dst, send_sem=r_send.at[n, stage], recv_sem=r_recv.at[n, stage],
            device_id=peer, device_id_type=mesh_id,
        )

    def stage_a(n, x, a):
        return exchange(half(x, 1 - vc), a, n, 0, c_peer)

    def stage_b(n, x, b):
        return exchange(half(x, vc), b, n, 1, y_peer)

    def stage_c(n, f):
        return exchange(half(f, vc), half(f, vc), n, 2, c_peer)

    def stage_c_arrival(n, f):
        return exchange(half(f, 1 - vc), half(f, 1 - vc), n, 2, c_peer)

    def a_to_b(n, x, a, b):
        stage_a(n, x, a).wait_recv()
        own = half(x, vc)
        own[...] = own[...] + a[...]
        stage_b(n, x, b).start()

    def b_to_c(n, x, b, f):
        stage_b(n, x, b).wait_recv()
        half(f, vc)[...] = half(x, vc)[...] + b[...]
        stage_c(n, f).start()

    def begin(c):
        for d in range(1, outer):
            z_copy(c, d).start()
        x_copy(c, 0).start()

    begin(0)
    for c in range(panels):
        table[c, rows_of(zi, xi)] = sent_ref[c]

    quarter = cols_ref.shape[1] // 4

    def ordered(c):
        place = pos_ref[c]
        count = pair_count * slots
        hit = lax.broadcasted_iota(jnp.int32, (width, count), 1) == place
        pick = jnp.where(hit, 1.0, 0.0).astype(BF16)
        nn = ((1,), (0,))
        high, low = split2(table[c, :, :depth])
        p_high[c] = dot(pick, high, nn).astype(BF16)
        p_low[c] = dot(pick, low, nn).astype(BF16)
        th, tm, tl = split3(table[c, :, depth:])
        return dot(pick, th, nn) + dot(pick, tm, nn) + dot(pick, tl, nn)

    def place_share(share, lanes):
        tiles = []
        for q in range(lanes // quarter):
            tiles.append(jnp.where(vec == q, share, 0.0))
        return jnp.concatenate(tiles, axis=1)

    forward(0)
    begin(1)
    finish_gather(0)
    share = ordered(0)
    rows0 = (p_high[0], p_low[0])
    x1[...] = place_share(share, width) - dot_nt(rows0, rows0)
    stage_a(0, x1, a1).start()
    a_to_b(0, x1, a1, b1)
    forward(1)
    b_to_c(0, x1, b1, f1)
    stage_c_arrival(0, f1).wait_recv()

    block = f1[...]
    set_work(work1, inv1, 0.5 * (block + block.T))
    band = eliminate(work1, inv1, 0, 4, start_band(work1))

    finish_gather(1)
    share = ordered(1)
    rows0 = (p_high[0], p_low[0])
    rows1 = (p_high[1], p_low[1])
    known = jnp.concatenate([dot_nt(rows1, rows0), dot_nt(rows1, rows1)], axis=1)
    x2[...] = place_share(share, 2 * width) - known
    stage_a(1, x2, a2).start()
    own = split2(prev_ref[...])
    x3[:, :width] = dot_nt(own, rows0)
    x3[:, width:] = dot_nt(own, rows1)
    stage_a(2, x3, a3).start()
    a_to_b(1, x2, a2, b2)
    band = eliminate(work1, inv1, 1, 4, band)
    a_to_b(2, x3, a3, b3)
    band = eliminate(work1, inv1, 2, 4, band)
    b_to_c(1, x2, b2, f2)
    band = eliminate(work1, inv1, 3, 4, band)
    stage_c_arrival(1, f2).wait_recv()

    inverse1 = split2(inv1[...])
    cross = split2(dot_nt(split2(f2[:, :width]), inverse1))
    block = f2[:, width:] - dot_nt(cross, cross)
    set_work(work2, inv2, 0.5 * (block + block.T))
    band = eliminate(work2, inv2, 0, 4, start_band(work2))
    band = eliminate(work2, inv2, 1, 4, band)
    b_to_c(2, x3, b3, f3)
    band = eliminate(work2, inv2, 2, 4, band)
    stage_c_arrival(2, f3).wait_recv()
    new1 = dot_nt(split2(cols_ref[:, :width] - f3[:, :width]), inverse1)
    out_ref[:, :width] = new1
    rest = cols_ref[:, width:] - f3[:, width:] - dot_nt(split2(new1), cross)
    band = eliminate(work2, inv2, 3, 4, band)
    out_ref[:, width:] = dot_nt(split2(rest), split2(inv2[...]))

    for c in range(panels):
        for d in range(1, outer):
            z_copy(c, d).wait_send()
        for d in range(outer):
            x_copy(c, d).wait_send()
    for n, (x, a, b, f) in enumerate(((x1, a1, b1, f1), (x2, a2, b2, f2), (x3, a3, b3, f3))):
        stage_a(n, x, a).wait_send()
        stage_b(n, x, b).wait_send()
        stage_c(n, f).wait_send()


def body(prev_vectors, columns, pivots):
    slab_rows, depth = prev_vectors.shape
    panels, width = pivots.shape
    pair_count = lax.axis_size("pairs")
    slots = max(8, 2 * width // pair_count)
    me = lax.axis_index("pairs")
    vec = lax.axis_index("vecs")
    owners = lax.div(pivots, jnp.int32(slab_rows))
    order = jnp.arange(width, dtype=jnp.int32)
    earlier = (owners[:, :, None] == owners[:, None, :]) & (order[None, None, :] < order[None, :, None])
    rank = jnp.sum(earlier.astype(jnp.int32), axis=2)
    place = owners * slots + rank
    wanted = me * slots + jnp.arange(slots, dtype=jnp.int32)
    hit = place[:, None, :] == wanted[None, :, None]
    local = jnp.sum(jnp.where(hit, (pivots - me * slab_rows)[:, None, :], 0), axis=2).reshape(-1)
    quarter = columns.shape[1] // lax.axis_size("vecs")
    share = lax.dynamic_slice_in_dim(columns[local], vec * quarter, quarter, 1)
    sent = jnp.concatenate([prev_vectors[local], share], axis=1)
    sent = sent.reshape(panels, slots, depth + quarter)
    count = pair_count * slots
    outer = pair_count // 2

    def vmem(*shape, dtype=F32):
        return pltpu.VMEM(shape, dtype)

    def reduced(rows, lanes):
        return [vmem(rows, lanes), vmem(rows // 2, lanes), vmem(rows // 2, lanes), vmem(rows, lanes)]

    scratch = [
        vmem(panels, count, depth + quarter),
        vmem(panels, width, depth, dtype=BF16),
        vmem(panels, width, depth, dtype=BF16),
        *reduced(width, width),
        *reduced(width, 2 * width),
        *reduced(slab_rows, 2 * width),
        vmem(width, 2 * width), vmem(width, width),
        vmem(width, 2 * width), vmem(width, width),
        pltpu.SemaphoreType.DMA((panels, outer)),
        pltpu.SemaphoreType.DMA((panels, outer)),
        pltpu.SemaphoreType.DMA((panels, outer)),
        pltpu.SemaphoreType.DMA((panels, outer)),
        pltpu.SemaphoreType.DMA((3, 3)),
        pltpu.SemaphoreType.DMA((3, 3)),
    ]
    whole = pl.BlockSpec(memory_space=pltpu.VMEM)
    return pl.pallas_call(
        functools.partial(kernel, pair_count),
        out_shape=jax.ShapeDtypeStruct((slab_rows, panels * width), F32),
        in_specs=[whole] * 4,
        out_specs=whole,
        scratch_shapes=scratch,
        compiler_params=pltpu.CompilerParams(
            collective_id=0, has_side_effects=True, vmem_limit_bytes=48 * 1024 * 1024
        ),
    )(sent, place[:, :, None], prev_vectors, columns)


def solution(mesh):
    placed = (P("pairs", "vecs"), P("pairs", None), P())
    return jax.shard_map(
        body, mesh=mesh, in_specs=placed, out_specs=P("pairs", None), check_vma=False
    )
```

```python
import functools

import jax
import jax.numpy as jnp
from jax import lax
from jax.experimental import pallas as pl
from jax.experimental.pallas import tpu as pltpu
from jax.sharding import PartitionSpec as P

F32 = jnp.float32
BF16 = jnp.bfloat16
STEP = 16


def split2(x):
    high = x.astype(BF16)
    return high, (x - high.astype(F32)).astype(BF16)


def split3(x):
    high = x.astype(BF16)
    rest = x - high.astype(F32)
    mid = rest.astype(BF16)
    return high, mid, (rest - mid.astype(F32)).astype(BF16)


def dot(a, b, dims):
    return lax.dot_general(a, b, (dims, ((), ())), preferred_element_type=F32)


def dot_nt(a, b):
    nt = ((1,), (1,))
    return dot(a[0], b[0], nt) + (dot(a[0], b[1], nt) + dot(a[1], b[0], nt))


def live_tiles(size, row):
    return range(row // 128, size // 128 + row // 128 + 1)


def start_band(work):
    return {t: work[:STEP, t * 128 : t * 128 + 128] for t in live_tiles(work.shape[0], 0)}


def inverse_of(x):
    guess = pl.reciprocal(x, approx=True)
    guess = guess * (2.0 - x * guess)
    return guess * (2.0 - x * guess)


def eliminate(work, inverse, chunk, chunks, band):
    size = work.shape[0]
    parts = size // 128
    per = size // STEP // chunks
    row_ids = lax.broadcasted_iota(jnp.int32, (STEP, 128), 0)
    for g in range(chunk * per, (chunk + 1) * per):
        row = g * STEP
        lane = row % 128
        names = live_tiles(size, row)
        tiles = [band[t] for t in names]
        cols = [jnp.broadcast_to(tiles[0][:, lane + j : lane + j + 1], (STEP, 128)) for j in range(STEP)]
        diag = jnp.ones((STEP, 128), F32)
        for k in range(0, STEP, 2):
            p, q = cols[k], cols[k + 1]
            a, b, c = p[k : k + 1, :], p[k + 1 : k + 2, :], q[k + 1 : k + 2, :]
            over_a = inverse_of(a)
            over_det = inverse_of(a * c - b * b)
            ratio = b * over_a
            diag = jnp.where(row_ids == k, a, jnp.where(row_ids == k + 1, c - b * ratio, diag))
            first_mult = jnp.where(row_ids > k + 1, p * over_a, 0.0)
            second_mult = jnp.where(row_ids > k + 1, (q - ratio * p) * (a * over_det), 0.0)
            pair_mult = jnp.where(row_ids == k + 1, ratio, first_mult)

            def step(x):
                top = x[k : k + 1, :]
                low = x[k + 1 : k + 2, :] - ratio * top
                return x - pair_mult * top - second_mult * low

            for j in range(k + 2, STEP):
                cols[j] = step(cols[j])
            tiles = [step(t) for t in tiles]
        scale = lax.rsqrt(diag)
        tiles = [t * scale for t in tiles]
        for t, tile in zip(names, tiles):
            if t >= parts:
                inverse[row : row + STEP, (t - parts) * 128 : (t - parts) * 128 + 128] = tile
        after = row + STEP
        if after == size:
            return None
        lane0 = names[0] * 128
        lane1 = lane0 + 128 * len(tiles)
        h, m, l = split3(jnp.concatenate(tiles, axis=1))
        left = jnp.concatenate([h, h, m, h, l, m], axis=0)
        right = jnp.concatenate([h, m, h, l, h, m], axis=0)
        near = dot(left[:, after - lane0 : after + STEP - lane0], right, ((0,), (0,)))
        band = {}
        for t in live_tiles(size, after):
            band[t] = work[after : after + STEP, t * 128 : t * 128 + 128]
            if t in names:
                band[t] = band[t] - near[:, t * 128 - lane0 : t * 128 - lane0 + 128]
        rest = after + STEP
        if rest < size:
            far = dot(left[:, rest - lane0 : size - lane0], right, ((0,), (0,)))
            work[rest:, lane0:lane1] = work[rest:, lane0:lane1] - far
    return band


def set_work(work, inverse, symmetric):
    size = symmetric.shape[0]
    rows = lax.broadcasted_iota(jnp.int32, (size, size), 0)
    lanes = lax.broadcasted_iota(jnp.int32, (size, size), 1)
    diagonal = jnp.where(rows == lanes, symmetric, 0.0)
    down = lax.rsqrt(jnp.sum(diagonal, axis=1, keepdims=True))
    along = lax.rsqrt(jnp.sum(diagonal, axis=0, keepdims=True))
    work[:, :size] = symmetric * down * along
    work[:, size:] = jnp.where(rows == lanes, down, 0.0)
    inverse[...] = jnp.zeros_like(inverse)


def kernel(
    pair_count, sent_ref, pos_ref, prev_ref, cols_ref, out_ref,
    table, p_high, p_low,
    x1, a1, b1, f1, x2, a2, b2, f2, x3, a3, b3, f3, x4, a4, b4, f4,
    work1, inv1, work2, inv2,
    z_send, z_recv, x_send, x_recv, r_send, r_recv,
):
    panels, slots, _ = sent_ref.shape
    depth = prev_ref.shape[1]
    width = cols_ref.shape[1] // panels
    outer = pair_count // 2
    me = lax.axis_index("pairs")
    vec = lax.axis_index("vecs")
    zi, xi = me // 2, lax.rem(me, 2)
    vy, vc = vec // 2, lax.rem(vec, 2)
    x_peer = {"pairs": zi * 2 + 1 - xi}
    c_peer = {"vecs": vy * 2 + 1 - vc}
    y_peer = {"vecs": (1 - vy) * 2 + vc}
    z_peers = [{"pairs": lax.rem(zi + d, outer) * 2 + xi} for d in range(1, outer)]
    mesh_id = pl.DeviceIdType.MESH

    barrier = pltpu.get_barrier_semaphore()
    everyone = [x_peer, c_peer, y_peer] + z_peers
    for peer in everyone:
        pl.semaphore_signal(barrier, inc=1, device_id=peer, device_id_type=mesh_id)
    pl.semaphore_wait(barrier, len(everyone))

    def rows_of(z, x):
        return pl.ds(pl.multiple_of((z * 2 + x) * slots, slots), slots)

    def z_copy(c, d):
        return pltpu.make_async_remote_copy(
            src_ref=sent_ref.at[c], dst_ref=table.at[c, rows_of(zi, xi)],
            send_sem=z_send.at[c, d], recv_sem=z_recv.at[c, d],
            device_id=z_peers[d - 1], device_id_type=mesh_id,
        )

    def z_arrival(c, d):
        return pltpu.make_async_remote_copy(
            src_ref=sent_ref.at[c], dst_ref=table.at[c, rows_of(lax.rem(zi + outer - d, outer), xi)],
            send_sem=z_send.at[c, d], recv_sem=z_recv.at[c, d],
            device_id=z_peers[d - 1], device_id_type=mesh_id,
        )

    def x_copy(c, d):
        rows = rows_of(lax.rem(zi + outer - d, outer), xi)
        return pltpu.make_async_remote_copy(
            src_ref=sent_ref.at[c] if d == 0 else table.at[c, rows], dst_ref=table.at[c, rows],
            send_sem=x_send.at[c, d], recv_sem=x_recv.at[c, d],
            device_id=x_peer, device_id_type=mesh_id,
        )

    def x_arrival(c, d):
        rows = rows_of(lax.rem(zi + outer - d, outer), 1 - xi)
        return pltpu.make_async_remote_copy(
            src_ref=sent_ref.at[c], dst_ref=table.at[c, rows],
            send_sem=x_send.at[c, d], recv_sem=x_recv.at[c, d],
            device_id=x_peer, device_id_type=mesh_id,
        )

    def forward(c):
        for d in range(1, outer):
            z_arrival(c, d).wait_recv()
            x_copy(c, d).start()

    def finish_gather(c):
        for d in range(outer):
            x_arrival(c, d).wait_recv()

    def half(ref, which):
        count = ref.shape[0] // 2
        return ref.at[pl.ds(pl.multiple_of(which * count, count), count)]

    def exchange(src, dst, n, stage, peer):
        return pltpu.make_async_remote_copy(
            src_ref=src, dst_ref=dst, send_sem=r_send.at[n, stage], recv_sem=r_recv.at[n, stage],
            device_id=peer, device_id_type=mesh_id,
        )

    def stage_a(n, x, a):
        return exchange(half(x, 1 - vc), a, n, 0, c_peer)

    def stage_b(n, x, b):
        return exchange(half(x, vc), b, n, 1, y_peer)

    def stage_c(n, f):
        return exchange(half(f, vc), half(f, vc), n, 2, c_peer)

    def stage_c_arrival(n, f):
        return exchange(half(f, 1 - vc), half(f, 1 - vc), n, 2, c_peer)

    def a_to_b(n, x, a, b):
        stage_a(n, x, a).wait_recv()
        own = half(x, vc)
        own[...] = own[...] + a[...]
        stage_b(n, x, b).start()

    def b_to_c(n, x, b, f):
        stage_b(n, x, b).wait_recv()
        half(f, vc)[...] = half(x, vc)[...] + b[...]
        stage_c(n, f).start()

    def begin(c):
        for d in range(1, outer):
            z_copy(c, d).start()
        x_copy(c, 0).start()

    begin(0)
    for c in range(panels):
        table[c, rows_of(zi, xi)] = sent_ref[c]

    quarter = cols_ref.shape[1] // 4

    def ordered(c):
        place = pos_ref[c]
        count = pair_count * slots
        hit = lax.broadcasted_iota(jnp.int32, (width, count), 1) == place
        pick = jnp.where(hit, 1.0, 0.0).astype(BF16)
        nn = ((1,), (0,))
        high, low = split2(table[c, :, :depth])
        p_high[c] = dot(pick, high, nn).astype(BF16)
        p_low[c] = dot(pick, low, nn).astype(BF16)
        th, tm, tl = split3(table[c, :, depth:])
        return dot(pick, th, nn) + dot(pick, tm, nn) + dot(pick, tl, nn)

    def place_share(share, lanes):
        tiles = []
        for q in range(lanes // quarter):
            tiles.append(jnp.where(vec == q, share, 0.0))
        return jnp.concatenate(tiles, axis=1)

    forward(0)
    begin(1)
    finish_gather(0)
    share = ordered(0)
    rows0 = (p_high[0], p_low[0])
    x1[...] = place_share(share, width) - dot_nt(rows0, rows0)
    stage_a(0, x1, a1).start()
    own = split2(prev_ref[...])
    x3[...] = dot_nt(own, rows0)
    a_to_b(0, x1, a1, b1)
    stage_a(2, x3, a3).start()
    forward(1)
    b_to_c(0, x1, b1, f1)
    a_to_b(2, x3, a3, b3)
    stage_c_arrival(0, f1).wait_recv()

    block = f1[...]
    set_work(work1, inv1, 0.5 * (block + block.T))
    band = eliminate(work1, inv1, 0, 4, start_band(work1))
    band = eliminate(work1, inv1, 1, 4, band)

    finish_gather(1)
    share = ordered(1)
    rows0 = (p_high[0], p_low[0])
    rows1 = (p_high[1], p_low[1])
    known = jnp.concatenate([dot_nt(rows1, rows0), dot_nt(rows1, rows1)], axis=1)
    x2[...] = place_share(share, 2 * width) - known
    stage_a(1, x2, a2).start()
    own = split2(prev_ref[...])
    x4[...] = dot_nt(own, rows1)
    a_to_b(1, x2, a2, b2)
    b_to_c(2, x3, b3, f3)
    stage_a(3, x4, a4).start()
    band = eliminate(work1, inv1, 2, 4, band)
    band = eliminate(work1, inv1, 3, 4, band)
    b_to_c(1, x2, b2, f2)
    a_to_b(3, x4, a4, b4)
    inverse1 = split2(inv1[...])
    stage_c_arrival(2, f3).wait_recv()
    stage_c_arrival(1, f2).wait_recv()

    cross = split2(dot_nt(split2(f2[:, :width]), inverse1))
    block = f2[:, width:] - dot_nt(cross, cross)
    set_work(work2, inv2, 0.5 * (block + block.T))
    band = eliminate(work2, inv2, 0, 4, start_band(work2))
    new1 = dot_nt(split2(cols_ref[:, :width] - f3[...]), inverse1)
    out_ref[:, :width] = new1
    band = eliminate(work2, inv2, 1, 4, band)
    rest = cols_ref[:, width:] - dot_nt(split2(new1), cross)
    band = eliminate(work2, inv2, 2, 4, band)
    b_to_c(3, x4, b4, f4)
    band = eliminate(work2, inv2, 3, 4, band)
    stage_c_arrival(3, f4).wait_recv()
    out_ref[:, width:] = dot_nt(split2(rest - f4[...]), split2(inv2[...]))

    reductions = (
        (x1, a1, b1, f1), (x2, a2, b2, f2), (x3, a3, b3, f3), (x4, a4, b4, f4),
    )
    for c in range(panels):
        for d in range(1, outer):
            z_copy(c, d).wait_send()
        for d in range(outer):
            x_copy(c, d).wait_send()
    for n, (x, a, b, f) in enumerate(reductions):
        stage_a(n, x, a).wait_send()
        stage_b(n, x, b).wait_send()
        stage_c(n, f).wait_send()


def body(prev_vectors, columns, pivots):
    slab_rows, depth = prev_vectors.shape
    panels, width = pivots.shape
    pair_count = lax.axis_size("pairs")
    slots = max(8, 2 * width // pair_count)
    me = lax.axis_index("pairs")
    vec = lax.axis_index("vecs")
    owners = lax.div(pivots, jnp.int32(slab_rows))
    order = jnp.arange(width, dtype=jnp.int32)
    earlier = (owners[:, :, None] == owners[:, None, :]) & (order[None, None, :] < order[None, :, None])
    rank = jnp.sum(earlier.astype(jnp.int32), axis=2)
    place = owners * slots + rank
    wanted = me * slots + jnp.arange(slots, dtype=jnp.int32)
    hit = place[:, None, :] == wanted[None, :, None]
    local = jnp.sum(jnp.where(hit, (pivots - me * slab_rows)[:, None, :], 0), axis=2).reshape(-1)
    quarter = columns.shape[1] // lax.axis_size("vecs")
    share = lax.dynamic_slice_in_dim(columns[local], vec * quarter, quarter, 1)
    sent = jnp.concatenate([prev_vectors[local], share], axis=1)
    sent = sent.reshape(panels, slots, depth + quarter)
    count = pair_count * slots
    outer = pair_count // 2

    def vmem(*shape, dtype=F32):
        return pltpu.VMEM(shape, dtype)

    def reduced(rows, lanes):
        return [vmem(rows, lanes), vmem(rows // 2, lanes), vmem(rows // 2, lanes), vmem(rows, lanes)]

    scratch = [
        vmem(panels, count, depth + quarter),
        vmem(panels, width, depth, dtype=BF16),
        vmem(panels, width, depth, dtype=BF16),
        *reduced(width, width),
        *reduced(width, 2 * width),
        *reduced(slab_rows, width),
        *reduced(slab_rows, width),
        vmem(width, 2 * width), vmem(width, width),
        vmem(width, 2 * width), vmem(width, width),
        pltpu.SemaphoreType.DMA((panels, outer)),
        pltpu.SemaphoreType.DMA((panels, outer)),
        pltpu.SemaphoreType.DMA((panels, outer)),
        pltpu.SemaphoreType.DMA((panels, outer)),
        pltpu.SemaphoreType.DMA((4, 3)),
        pltpu.SemaphoreType.DMA((4, 3)),
    ]
    whole = pl.BlockSpec(memory_space=pltpu.VMEM)
    return pl.pallas_call(
        functools.partial(kernel, pair_count),
        out_shape=jax.ShapeDtypeStruct((slab_rows, panels * width), F32),
        in_specs=[whole] * 4,
        out_specs=whole,
        scratch_shapes=scratch,
        compiler_params=pltpu.CompilerParams(
            collective_id=0, has_side_effects=True, vmem_limit_bytes=48 * 1024 * 1024
        ),
    )(sent, place[:, :, None], prev_vectors, columns)


def solution(mesh):
    placed = (P("pairs", "vecs"), P("pairs", None), P())
    return jax.shard_map(
        body, mesh=mesh, in_specs=placed, out_specs=P("pairs", None), check_vma=False
    )
```
